32 devices in a mesh: row: 4 (over y, x), col: 8 (over z, core).
Axes of the slice: x: 2, y: 2, z: 4, core: 2. Of those that a mesh axis runs over, the one named last changes fastest.
Arguments:
- grad: float32 [7168, 8192], P(('row', 'col')), may hold values from -60 to 60
- momentum: float32 [7168, 8192], P(('row', 'col')), may hold values from -6 to 6
Outputs:
- update: bfloat16 [7168, 8192], P(('row', 'col'))
- new_momentum: float32 [7168, 8192], P(('row', 'col'))
The draws below stay inside these ranges and needn't reach their ends.
All inputs are finite; a program needn't handle non-finite values.
Results may differ from the reference program's by a relative error of at most 0.02.
Values may be sent and summed in bfloat16 or wider, within the bound.
No kernel may reach another device: no remote copies, remote signals or barrier semaphores. Data moves between devices by JAX's collectives and lax.ppermute only.
A program may use at most 128 MiB of HBM per device.

```python
import math
import jax
import jax.numpy as jnp
from jax import lax

M = 7168
N = 8192
NB = 1024


def draw_grad(key, part):
    keys = jax.random.split(key, 3)
    base_vals = jnp.clip(jax.random.normal(keys[0], (M, N), jnp.float32), -4.0, 4.0)
    row_scale = jnp.exp(jax.random.uniform(keys[1], (M, 1), jnp.float32, 0.0, math.log(10.0)))
    col_scale = jnp.exp(jax.random.uniform(keys[2], (1, N), jnp.float32, 0.0, math.log(10.0)))
    trend = jnp.exp(math.log(3.0) * jnp.arange(M, dtype=jnp.float32) / M).reshape(M, 1)
    return (0.05 * base_vals * row_scale * col_scale * trend).astype(jnp.float32)


def level_of(stream_key, extent, cuts, low, largest):
    gain, own = 1.0, jax.random.fold_in(stream_key, 6)
    for dim, blocks in cuts:
        steps = jnp.exp(jax.random.uniform(jax.random.fold_in(own, dim), (blocks,), jnp.float32, low / len(cuts), largest / len(cuts)))
        gain = gain * jnp.repeat(steps, extent[dim] // blocks).reshape([-1 if axis == dim else 1 for axis in range(len(extent))])
    return gain


def gaussian(own_key, dims, width, reach, cuts=(), held_as=jnp.bfloat16):
    level = level_of(own_key, dims, cuts, -0.22, 0.18) if cuts else 1.0
    array = jax.random.normal(own_key, dims, jnp.float32) * width * level
    return jnp.minimum(jnp.maximum(array, -reach), reach).astype(held_as)


def setup_inputs(seed: int = 0) -> dict:
    arg_keys = jax.random.split(jax.random.key(seed), 3)
    return {
        "grad": draw_grad(jax.random.fold_in(arg_keys[2], 71), 0),
        "momentum": gaussian(arg_keys[1], (M, N), 1.0, 6.0, ((0, 32),), jnp.float32),
    }


momentum_coef = 0.95
rms_target = 0.4
coef_a = 3.4445
coef_b = -4.775
coef_c = 2.0315

def reference(grad, momentum):
    new_momentum = momentum_coef * momentum + grad
    direction = grad + momentum_coef * new_momentum
    sumsq = jnp.sum(direction * direction)
    factor = rms_target * jnp.sqrt(jnp.float32(M)) / (jnp.sqrt(sumsq) + 1e-07)
    start = (direction * factor).astype(jnp.bfloat16)
    start_wide = start.astype(jnp.float32)
    groups = start_wide.reshape(M, N // NB, NB).transpose(1, 0, 2)

    def add_group(carry, group):
        partial_gram = jnp.dot(group, group.T, precision=lax.Precision.HIGHEST)
        rounded = lax.optimization_barrier(partial_gram.astype(jnp.bfloat16))
        return (carry + rounded.astype(jnp.float32), None)
    summed, unused = lax.scan(add_group, jnp.zeros((M, M), jnp.float32), groups)
    gram = lax.optimization_barrier(summed.astype(jnp.bfloat16)).astype(jnp.float32)
    first = jnp.dot(gram, start_wide, precision=lax.Precision.HIGHEST)
    first_round = lax.optimization_barrier(first.astype(jnp.bfloat16)).astype(jnp.float32)
    second = jnp.dot(gram, first_round, precision=lax.Precision.HIGHEST)
    scale_out = 0.2 * jnp.sqrt(jnp.float32(max(M, N)))
    result = coef_a * start_wide + coef_b * first + coef_c * second
    return ((result * scale_out).astype(jnp.bfloat16), new_momentum)
```

```python
import math

import jax
import jax.numpy as jnp
from jax import lax
from jax.sharding import PartitionSpec as P

momentum_coef = 0.95
rms_target = 0.4
coef_a = 3.4445
coef_b = -4.775
coef_c = 2.0315
CHUNKS = 2
F32 = jnp.float32
BF16 = jnp.bfloat16


def xor_pairs(size, distance):
    return [(i, i ^ distance) for i in range(size)]


def shift_pairs(size, distance):
    return [(i, (i + distance) % size) for i in range(size)]


def low_bit(distance):
    return (distance & -distance).bit_length() - 1


def shards(grad, momentum):
    n_row, n_col = lax.axis_size("row"), lax.axis_size("col")
    n_ring = n_col // 2
    row, col = lax.axis_index("row"), lax.axis_index("col")
    ring, core = col // 2, col % 2
    rows, n_in = grad.shape
    half = rows // 2
    width = n_in // n_col
    tall = half * n_col
    m_total = rows * n_row * n_col

    def across(value, distance):
        return lax.ppermute(value, "row", xor_pairs(n_row, distance))

    def other_core(value):
        return lax.ppermute(value, "col", xor_pairs(n_col, 1))

    def next_in_ring(value):
        return lax.ppermute(value, "col", shift_pairs(n_col, 2))

    new_momentum = momentum_coef * momentum + grad
    direction = grad + momentum_coef * new_momentum
    raw = direction.astype(BF16)

    sumsq = jnp.sum(direction * direction).reshape(1, 1)
    step = 1
    while step < n_col:
        sumsq = sumsq + lax.ppermute(sumsq, "col", xor_pairs(n_col, step))
        step *= 2
    step = 1
    while step < n_row:
        sumsq = sumsq + across(sumsq, step)
        step *= 2
    factor = rms_target * math.sqrt(m_total) / (jnp.sqrt(sumsq) + 1e-07)
    factor_sq = (factor * factor).reshape(1, 1, 1)

    own, others = [], [{}, {}]
    for h in range(2):
        block = lax.all_to_all(
            raw[h * half : (h + 1) * half], "col", split_axis=1, concat_axis=0, tiled=True
        )
        own.append(block)
        if n_row == 4:
            others[h][1] = across(block, 1)
            others[h][2] = across(block, 2)
            others[h][3] = across(others[h][1], 2) if h == 0 else across(others[h][2], 1)
        else:
            for d in range(1, n_row):
                others[h][d] = across(block, d)

    def swapped(first_half, second_half, d):
        upper = ((row >> low_bit(d)) & 1) == 1
        return jnp.stack(
            [
                jnp.where(upper, second_half, first_half),
                jnp.where(upper, first_half, second_half),
            ]
        )

    own2 = jnp.stack(own)
    mixed = {d: swapped(others[0][d], others[1][d], d) for d in range(1, n_row)}

    def gram_term(left, right):
        term = lax.dot_general(left, right, (((2,), (2,)), ((0,), (0,))), preferred_element_type=F32)
        return (term * factor_sq).astype(BF16)

    def reduce_ring(term):
        count = term.shape[0]
        pieces = term.reshape(count, n_ring, 2, half, tall)
        kept = lax.dynamic_index_in_dim(pieces, core, 2, keepdims=False)
        sent = lax.dynamic_index_in_dim(pieces, 1 - core, 2, keepdims=False)
        summed = (kept.astype(F32) + other_core(sent).astype(F32)).astype(BF16)

        def part(index):
            return lax.dynamic_index_in_dim(summed, index % n_ring, 1, keepdims=False)

        total = part(ring + n_ring - 1)
        for t in range(1, n_ring):
            total = next_in_ring(total).astype(F32) + part(ring + n_ring - 1 - t).astype(F32)
            total = total.astype(BF16)
        return total

    def gather_ring(piece):
        found = [piece]
        for _ in range(1, n_ring):
            found.append(next_in_ring(found[-1]))
        return found

    def assemble(found):
        count = found[0].shape[0]
        full = jnp.zeros((count, n_ring, 2, half, tall), BF16)
        partner = other_core(jnp.stack(found))
        for k, piece in enumerate(found):
            place = (ring - k + n_ring) % n_ring
            full = lax.dynamic_update_slice(full, piece[:, None, None], (0, place, core, 0, 0))
            full = lax.dynamic_update_slice(
                full, partner[k][:, None, None], (0, place, 1 - core, 0, 0)
            )
        return full.reshape(count, tall, tall)

    def exchange(found, d):
        upper = ((row >> low_bit(d)) & 1) == 1
        return [across(jnp.where(upper, piece[::-1], piece), d) for piece in found]

    corner = gather_ring(reduce_ring(gram_term(own2, own2)))
    side = gather_ring(reduce_ring(gram_term(own2[:1], own2[1:])))
    corner, side = assemble(corner), assemble(side)[0]
    near, far = {}, {}
    for d in range(1, n_row):
        found = gather_ring(reduce_ring(gram_term(own2, mixed[d])))
        near[d] = assemble(found)
        far[d] = assemble(exchange(found, d))

    def times_gram(mine, theirs):
        plain = (((2,), (1,)), ((0,), (0,)))
        turned = (((1,), (1,)), ((0,), (0,)))
        total = lax.dot_general(corner, mine, plain, preferred_element_type=F32)
        total = total + jnp.stack(
            [
                lax.dot_general(side, mine[1], (((1,), (0,)), ((), ())), preferred_element_type=F32),
                lax.dot_general(side, mine[0], (((0,), (0,)), ((), ())), preferred_element_type=F32),
            ]
        )
        for d in range(1, n_row):
            total = total + lax.dot_general(near[d], theirs[d], plain, preferred_element_type=F32)
            total = total + lax.dot_general(
                far[d], theirs[d][::-1], turned, preferred_element_type=F32
            )
        return total

    scale_out = 0.2 * math.sqrt(max(m_total, n_in))
    update = jnp.zeros((rows, n_in), BF16)
    part_width = width // CHUNKS
    for chunk in range(CHUNKS):
        cut = slice(chunk * part_width, (chunk + 1) * part_width)
        mine = own2[:, :, cut]
        first = times_gram(mine, {d: mixed[d][:, :, cut] for d in mixed})
        rounded = first.astype(BF16)
        if n_row == 4:
            got1, got2 = across(rounded, 1), across(rounded, 2)
            got = {1: got1, 2: got2, 3: (across(got1[0], 2), across(got2[1], 1))}
        else:
            got = {d: across(rounded, d) for d in range(1, n_row)}
        second = times_gram(rounded, {d: swapped(got[d][0], got[d][1], d) for d in got})
        result = coef_a * mine.astype(F32) + coef_b * first + coef_c * second
        block = (result * (factor * scale_out).reshape(1, 1, 1)).astype(BF16)
        block = block.reshape(2, n_col, half, part_width)
        for k in range(n_col):
            piece = lax.dynamic_index_in_dim(block, (col + k) % n_col, 1, keepdims=False)
            if k:
                piece = lax.ppermute(piece, "col", shift_pairs(n_col, k))
            source = (col - k + n_col) % n_col
            update = lax.dynamic_update_slice(
                update,
                piece.reshape(rows, part_width),
                (0, source * width + chunk * part_width),
            )
    return (update, new_momentum)


def solution(mesh):
    return jax.shard_map(
        shards,
        mesh=mesh,
        in_specs=(P(("row", "col"), None), P(("row", "col"), None)),
        out_specs=(P(("row", "col"), None), P(("row", "col"), None)),
        check_vma=False,
    )
```

```python
import math

import functools

import jax
import jax.numpy as jnp
from jax import lax
from jax.experimental import pallas as pl
from jax.experimental.pallas import tpu as pltpu
from jax.sharding import PartitionSpec as P

momentum_coef = 0.95
rms_target = 0.4
coef_a = 3.4445
coef_b = -4.775
coef_c = 2.0315
TILE = 256
VMEM = 56 * 1024 * 1024
F32 = jnp.float32
BF16 = jnp.bfloat16


def xor_pairs(size, distance):
    return [(i, i ^ distance) for i in range(size)]


def shift_pairs(size, distance):
    return [(i, (i + distance) % size) for i in range(size)]


def low_bit(distance):
    return (distance & -distance).bit_length() - 1


class Slots:
    def __init__(self):
        self.ended, self.noted = None, []

    def hold(self, value):
        return value if self.ended is None else lax.optimization_barrier((value, self.ended))[0]

    def note(self, value):
        self.noted.append(value)
        return value

    def close(self):
        if self.noted:
            self.ended = lax.optimization_barrier(tuple(self.noted))[0]
            self.noted = []


def direction_kernel(grad, momentum, new_momentum, upper, lower, sumsq, squares):
    lower_half, part = pl.program_id(0), pl.program_id(1)
    state = momentum_coef * momentum[...] + grad[...]
    new_momentum[...] = state
    direction = grad[...] + momentum_coef * state
    width = upper.shape[2]

    @pl.when((lower_half == 0) & (part == 0))
    def _():
        squares[...] = jnp.zeros_like(squares)

    for out, mine in ((upper, lower_half == 0), (lower, lower_half == 1)):

        @pl.when(mine)
        def _(out=out):
            for group in range(out.shape[0]):
                out[group] = direction[:, group * width : (group + 1) * width].astype(BF16)

    total = squares[...]
    for row in range(0, direction.shape[0], 8):
        rows = direction[row : row + 8]
        total = total + rows * rows
    squares[...] = total

    @pl.when((lower_half == 1) & (part == pl.num_programs(1) - 1))
    def _():
        sumsq[0, 0] = jnp.sum(squares[...])


def direction_step(grad, momentum, n_col):
    rows, n_in = grad.shape
    half, width = rows // 2, n_in // n_col
    if half % 16:
        state = momentum_coef * momentum + grad
        direction = grad + momentum_coef * state
        raw = direction.astype(BF16).reshape(2, half, n_col, width).transpose(0, 2, 1, 3)
        return state, raw[0], raw[1], jnp.sum(direction * direction).reshape(1, 1)
    parts = 2
    tile = pl.BlockSpec((half, n_in // parts), lambda i, j: (i, j))
    groups = (n_col // parts, half, width)
    return pl.pallas_call(
        direction_kernel,
        grid=(2, parts),
        in_specs=[tile, tile],
        out_specs=[
            tile,
            pl.BlockSpec(groups, lambda i, j: (jnp.where(i == 0, j, parts - 1), 0, 0)),
            pl.BlockSpec(groups, lambda i, j: (jnp.where(i == 0, 0, j), 0, 0)),
            pl.BlockSpec(memory_space=pltpu.SMEM),
        ],
        out_shape=[
            jax.ShapeDtypeStruct((rows, n_in), F32),
            jax.ShapeDtypeStruct((n_col, half, width), BF16),
            jax.ShapeDtypeStruct((n_col, half, width), BF16),
            jax.ShapeDtypeStruct((1, 1), F32),
        ],
        scratch_shapes=[pltpu.VMEM((8, n_in // parts), F32)],
        compiler_params=pltpu.CompilerParams(vmem_limit_bytes=VMEM),
    )(grad, momentum)


def absorb_kernel(n_ring, half, first_near, mirrored, seeded, scaled, *refs):
    places, refs = refs[0], refs[1:]
    if scaled:
        scale, refs = refs[0], refs[1:]
    near, refs = refs[: 2 * n_ring], refs[2 * n_ring :]
    if not mirrored:
        far, refs = refs[: 2 * n_ring], refs[2 * n_ring :]
    value, refs = refs[0], refs[1:]
    if seeded:
        before, refs = refs[0], refs[1:]
    block, total, refs = refs[0], refs[1], refs[2:]
    if scaled:
        rounded, refs = refs[0], refs[1:]
    turned, sems = refs
    tall = block.shape[0] // 2

    @pl.when(pl.program_id(0) == 0)
    def _():
        copies = []

        def place(source, target):
            copy = pltpu.make_async_copy(source, target, sems.at[len(copies)])
            copy.start()
            copies.append(copy)

        for k in range(2 * n_ring):
            at = pl.ds(pl.multiple_of(places[k], 16), half)
            below = pl.ds(pl.multiple_of(places[k] + tall, 16), half)
            place(near[k].at[first_near], block.at[at, pl.ds(0, tall)])
            place(near[k].at[first_near + 1], block.at[below, pl.ds(tall, tall)])
            if mirrored:
                place(near[k].at[first_near + 2], block.at[at, pl.ds(tall, tall)])
            else:
                place(far[k].at[0], turned.at[0, at])
                place(far[k].at[1], turned.at[1, at])
        for copy in copies:
            copy.wait()
        for j in range(0, tall, 128):
            if mirrored:
                block[pl.ds(tall + j, 128), pl.ds(0, tall)] = block[
                    pl.ds(0, tall), pl.ds(tall + j, 128)
                ].T
            else:
                block[pl.ds(j, 128), pl.ds(tall, tall)] = turned[0, :, pl.ds(j, 128)].T
                block[pl.ds(tall + j, 128), pl.ds(0, tall)] = turned[1, :, pl.ds(j, 128)].T

    result = jnp.dot(block[...], value[...], preferred_element_type=F32)
    if seeded:
        result = result + before[...]
    if scaled:
        result = result * scale[0]
        rounded[...] = result.astype(BF16)
    total[...] = result


def absorb(places, near, first_near, far, value, wide, before=None, scale=None):
    _, half, tall = near[0].shape
    tile = min(TILE, wide)
    whole = pl.BlockSpec(memory_space=pl.ANY)
    scalars = pl.BlockSpec(memory_space=pltpu.SMEM)
    column = pl.BlockSpec((2 * tall, tile), lambda n: (0, n))
    operands, specs = [places], [scalars]
    if scale is not None:
        operands.append(scale)
        specs.append(scalars)
    operands += [*near, *far, value]
    specs += [whole] * (len(near) + len(far)) + [column]
    if before is not None:
        operands.append(before)
        specs.append(column)
    shapes = [
        jax.ShapeDtypeStruct((2 * tall, 2 * tall), BF16),
        jax.ShapeDtypeStruct((2 * tall, wide), F32),
    ]
    out_specs = [pl.BlockSpec((2 * tall, 2 * tall), lambda n: (0, 0)), column]
    if scale is not None:
        shapes.append(jax.ShapeDtypeStruct((2 * tall, wide), BF16))
        out_specs.append(column)
    return pl.pallas_call(
        functools.partial(
            absorb_kernel,
            len(near) // 2,
            half,
            first_near,
            not far,
            before is not None,
            scale is not None,
        ),
        grid=(wide // tile,),
        in_specs=specs,
        out_specs=out_specs,
        out_shape=shapes,
        scratch_shapes=[
            pltpu.VMEM((2, tall, tall), BF16),
            pltpu.SemaphoreType.DMA((4 * len(near),)),
        ],
        compiler_params=pltpu.CompilerParams(vmem_limit_bytes=VMEM),
        cost_estimate=pl.CostEstimate(
            flops=8 * tall * tall * wide, bytes_accessed=30 * tall * tall, transcendentals=0
        ),
    )(*operands)


def shards(grad, momentum):
    n_row, n_col = lax.axis_size("row"), lax.axis_size("col")
    n_ring = n_col // 2
    row, col = lax.axis_index("row"), lax.axis_index("col")
    ring, core = col // 2, col % 2
    rows, n_in = grad.shape
    half = rows // 2
    width = n_in // n_col
    tall = half * n_col
    m_total = rows * n_row * n_col
    slots = Slots()

    def after(value, *others):
        return lax.optimization_barrier((value, *others))[0]

    def across(value, distance):
        return lax.ppermute(value, "row", xor_pairs(n_row, distance))

    def other_core(value):
        return lax.ppermute(value, "col", xor_pairs(n_col, 1))

    def next_in_ring(value):
        return lax.ppermute(value, "col", shift_pairs(n_col, 2))

    new_momentum, *raw_halves, sumsq = direction_step(grad, momentum, n_col)

    sumsq = sumsq + other_core(sumsq)
    step = 1
    while step < n_row:
        sumsq = sumsq + across(sumsq, step)
        step *= 2
    raw_halves[1] = after(raw_halves[1], sumsq)

    near = (1, 2) if n_row == 4 else tuple(range(1, n_row))
    own = []
    for h in range(2):
        block = lax.all_to_all(raw_halves[h], "col", split_axis=0, concat_axis=0)
        own.append(block.reshape(tall, width))
        if h == 0:
            others = [{d: across(own[0], d) for d in near}, {}]
    own[1] = after(own[1], *others[0].values())
    own2 = jnp.stack(own)
    cut = tall // 2

    def is_upper(d):
        return ((row >> low_bit(d)) & 1) == 1

    def swapped(first_half, second_half, d):
        return jnp.stack(
            [
                jnp.where(is_upper(d), second_half, first_half),
                jnp.where(is_upper(d), first_half, second_half),
            ]
        )

    own2 = jnp.stack(own)
    mixed = {}

    def gram_term(left, right):
        return lax.dot_general(
            left, right, (((2,), (2,)), ((0,), (0,))), preferred_element_type=F32
        ).astype(BF16)

    class Reduce:
        def __init__(self, terms):
            self.pieces = [term.reshape(-1, n_ring, 2, half, tall) for term in terms]
            self.parts = [self.part(t) for t in range(n_ring)]
            self.done = 0
            self.total = self.parts[0].astype(BF16)

        def part(self, t):
            index = (ring + n_ring - 1 - t) % n_ring
            sent, kept = self.pick(index, 1 - core), self.pick(index, core)
            return slots.note(kept.astype(F32) + other_core(sent).astype(F32))

        def pick(self, index, which):
            zero = jnp.zeros((), jnp.int32)
            picked = []
            for piece in self.pieces:
                sizes = (piece.shape[0], 1, 1, half, tall)
                part = lax.dynamic_slice(slots.hold(piece), (zero, index, which, zero, zero), sizes)
                picked.append(part.reshape(-1, half, tall))
            return picked[0] if len(picked) == 1 else jnp.concatenate(picked)

        def step(self):
            self.done += 1
            moved = slots.note(next_in_ring(slots.hold(self.total)))
            self.total = (moved.astype(F32) + self.parts[self.done]).astype(BF16)

    class Gather:
        def __init__(self, piece, distances):
            self.distances = distances
            self.found, self.partner = [piece], []
            self.crossed = {d: ([], []) for d in distances}
            self.left = list(enumerate(distances)) or [(0, 0)]

        @property
        def taken(self):
            return not self.left

        def complete(self):
            shared = [self.partner, *[theirs for _, theirs in self.crossed.values()]]
            return all(len(pieces) == n_ring for pieces in shared)

        def take_next(self, total, scale=None):
            i, d = self.left.pop(0)
            pieces = self.found + self.partner
            far = self.crossed[d][0] + self.crossed[d][1] if d else []
            value = flat(mixed[d] if d else own2)
            blocks[d], *made = take(pieces, 2 * i, far, value, total, None if self.left else scale)
            return made[0], made[1:]

        def step(self):
            self.found.append(slots.note(next_in_ring(slots.hold(self.found[-1]))))

        def share(self, held=True):
            hold = slots.hold if held else lambda value: value
            note = slots.note if held else lambda value: value
            for d in self.distances:
                mine, theirs = self.crossed[d]
                for part in mine[len(theirs) :]:
                    theirs.append(note(other_core(hold(part))))
            for piece in self.found[len(self.partner) :]:
                self.partner.append(note(other_core(hold(piece))))
                for i, d in enumerate(self.distances):
                    part = hold(piece[2 * i : 2 * i + 2])
                    part = jnp.where(is_upper(d), jnp.flip(part, 0), part)
                    self.crossed[d][0].append(note(across(part, d)))

    places = [(ring - k + n_ring) % n_ring for k in range(n_ring)]
    places = [(2 * place + core) * half for place in places] + [
        (2 * place + 1 - core) * half for place in places
    ]
    places = jnp.stack(places).astype(jnp.int32)
    n_in_line = 2 * tall
    wide = width // 2
    aligned = half % 16 == 0 and tall % 128 == 0

    def take(near, first_near, far, value, before=None, scale=None):
        if aligned:
            return absorb(places, near, first_near, far, value, wide, before, scale)

        def tiles(pieces):
            full = jnp.zeros((pieces[0].shape[0], tall, tall), BF16)
            for k, piece in enumerate(pieces):
                full = lax.dynamic_update_slice(full, piece, (0, places[k], 0))
            return full

        near = tiles([piece[first_near : first_near + (2 if far else 3)] for piece in near])
        b, c = tiles(far).transpose(0, 2, 1) if far else (near[2], near[2].T)
        block = jnp.concatenate(
            [jnp.concatenate([near[0], b], axis=1), jnp.concatenate([c, near[1]], axis=1)], axis=0
        )
        block = lax.optimization_barrier(block)
        total = jnp.dot(block, value[:, :wide], preferred_element_type=F32)
        total = total if before is None else total + before
        if scale is None:
            return block, total
        total = total * scale[0]
        return block, total, total.astype(BF16)

    def flat(value):
        return value.reshape(n_in_line, value.shape[-1])

    distances = list(range(1, n_row))
    groups = [distances[i : i + 2] for i in range(0, len(distances), 2)]
    blocks = {}
    moving = {}

    def move_second_half(part):
        for d in near:
            moving[d, part] = slots.note(across(slots.hold(own[1][part]), d))

    def move_to_diagonal(part):
        if n_row == 4:
            one, two = slots.hold(others[0][1][part]), slots.hold(moving[2, part])
            moving[3, 0, part] = slots.note(across(one, 2))
            moving[3, 1, part] = slots.note(across(two, 1))

    def make_term(d):
        if d in near:
            lower = jnp.concatenate([moving[d, part] for part in parts])
            upper = others[0][d]
        else:
            upper, lower = [jnp.concatenate([moving[3, h, part] for part in parts]) for h in range(2)]
        mixed[d] = swapped(slots.hold(upper), slots.hold(lower), d)
        return slots.note(gram_term(own2, mixed[d]))

    parts = (slice(0, cut), slice(cut, tall))
    move_second_half(parts[0])
    reduces = [[Reduce([gram_term(own2, own2), gram_term(own2[:1], own2[1:])]), []]]
    slots.close()
    gathers, terms = [], {}
    total, rounded = None, None
    waiting = [(d, 3 if d in near else 5) for d in distances]
    number = 2
    while reduces or waiting or terms or any(len(g.found) < n_ring for g in gathers):
        if number == 2:
            move_second_half(parts[1])
            step = 2
            sumsq = slots.hold(sumsq)
            while step < n_col:
                sumsq = sumsq + lax.ppermute(sumsq, "col", xor_pairs(n_col, step))
                step *= 2
            slots.note(sumsq)
        elif number in (3, 4):
            move_to_diagonal(parts[number - 3])
        for gather in gathers:
            gather.share()
        stepping = [run for run, _ in reduces][:2]
        stepping += [g for g in gathers if g.distances and len(g.found) < n_ring][: 2 - len(stepping)][:1]
        stepping += [g for g in gathers if not g.distances and len(g.found) < n_ring]
        for run in stepping:
            run.step()
        opened = None
        if groups and number >= 3:
            for group in groups[:1]:
                if all(d in terms for d in group):
                    opened = [Reduce([terms.pop(d) for d in group]), groups.pop(0)]
        if waiting and number >= waiting[0][1]:
            d = waiting.pop(0)[0]
            terms[d] = make_term(d)
        complete = [gather for gather in gathers if gather.complete() and not gather.taken]
        if complete and (groups or reduces or gathers[-1] is not complete[0]):
            total, rounded = complete[0].take_next(total)
            slots.note(total)
        slots.close()
        for pair in [pair for pair in reduces if pair[0].done == n_ring - 1]:
            gathers.append(Gather(pair[0].total, pair[1]))
            reduces.remove(pair)
        if opened:
            reduces.append(opened)
        number += 1
    factor = rms_target * math.sqrt(m_total) / (jnp.sqrt(sumsq) + 1e-07)
    factor_sq = factor * factor
    scale = factor_sq.reshape(1)
    for gather in gathers:
        gather.share()
    slots.close()
    for gather in gathers:
        gather.share(False)
    for gather in gathers:
        while not gather.taken:
            total, rounded = gather.take_next(total, scale if gather is gathers[-1] else None)

    def product(d, value):
        return jnp.dot(blocks[d], value, preferred_element_type=F32)

    left, right = slice(0, wide), slice(wide, 2 * wide)
    last = 0.0
    for d in [0, *distances]:
        value = after(flat(mixed[d] if d else own2), rounded[0])
        last = last + product(d, value[:, right])
    first = [total, last * factor_sq]
    rounds = [rounded[0].reshape(2, tall, wide), first[1].astype(BF16).reshape(2, tall, wide)]
    scale_out = 0.2 * math.sqrt(max(m_total, n_in))
    def send(value, *ties):
        value = after(value, *ties) if ties else value
        return {d: across(value, d) for d in near}

    def forward(found, tie):
        if n_row != 4:
            return ()
        one, two = after(found[1][0], tie), after(found[2][1], tie)
        return across(one, 2), across(two, 1)

    def nearby(value, found, tie):
        second = product(0, flat(after(value, tie)))
        for d in near:
            second = second + product(d, flat(swapped(*[after(v, tie) for v in found[d]], d)))
        return second

    def finish(side, second, corner, *ties):
        if corner:
            second = second + product(3, flat(swapped(*[after(v, *ties) for v in corner], 3)))
        mine = flat(own2)[:, (left, right)[side]].astype(F32)
        result = coef_a * mine + coef_b * first[side] + coef_c * (second * factor_sq)
        return (result * (factor * scale_out)).astype(BF16).reshape(2, n_col, half, wide)

    def send_back(block):
        return lax.all_to_all(block, "col", split_axis=1, concat_axis=1, tiled=True)

    found = [send(rounds[0])]
    ended = lax.optimization_barrier((rounds[1], *found[0].values()))[0]
    corner = forward(found[0], ended)
    second = nearby(rounds[0], found[0], ended)
    ended = lax.optimization_barrier((second, *corner))[0]
    found.append(send(rounds[1], ended))
    block = finish(0, second, corner, ended)
    ended = lax.optimization_barrier((block, *found[1].values()))[0]
    backs = [send_back(block)]
    corner = forward(found[1], ended)
    second = nearby(rounds[1], found[1], ended)
    ended = lax.optimization_barrier((second, backs[0], *corner))[0]
    backs.append(send_back(finish(1, second, corner, ended)))
    update = jnp.zeros((rows, n_in), BF16)
    for side, back in enumerate(backs):
        for source in range(n_col):
            piece = back[:, source].reshape(rows, wide)
            update = lax.dynamic_update_slice(update, piece, (0, source * width + side * wide))
    return (update, new_momentum)


def solution(mesh):
    return jax.shard_map(
        shards,
        mesh=mesh,
        in_specs=(P(("row", "col"), None), P(("row", "col"), None)),
        out_specs=(P(("row", "col"), None), P(("row", "col"), None)),
        check_vma=False,
    )
```

```python
import math

import functools

import jax
import jax.numpy as jnp
from jax import lax
from jax.experimental import pallas as pl
from jax.experimental.pallas import tpu as pltpu
from jax.sharding import PartitionSpec as P

momentum_coef = 0.95
rms_target = 0.4
coef_a = 3.4445
coef_b = -4.775
coef_c = 2.0315
TILE = 256
VMEM = 56 * 1024 * 1024
F32 = jnp.float32
BF16 = jnp.bfloat16


def xor_pairs(size, distance):
    return [(i, i ^ distance) for i in range(size)]


def shift_pairs(size, distance):
    return [(i, (i + distance) % size) for i in range(size)]


def low_bit(distance):
    return (distance & -distance).bit_length() - 1


class Slots:
    def __init__(self):
        self.ended, self.noted = None, []

    def hold(self, value):
        return value if self.ended is None else lax.optimization_barrier((value, self.ended))[0]

    def note(self, value):
        self.noted.append(value)
        return value

    def close(self):
        if self.noted:
            self.ended = lax.optimization_barrier(tuple(self.noted))[0]
            self.noted = []


def direction_kernel(grad, momentum, *refs):
    new_momentum, raw, sumsq, squares = refs[-4:]
    part = pl.program_id(0)
    state = momentum_coef * momentum[...] + grad[...]
    new_momentum[...] = state
    direction = grad[...] + momentum_coef * state
    width = raw.shape[2]
    for group in range(raw.shape[0]):
        raw[group] = direction[:, group * width : (group + 1) * width].astype(BF16)

    @pl.when(part == 0)
    def _():
        squares[...] = jnp.zeros_like(squares)

    total = squares[...]
    for row in range(0, direction.shape[0], 8):
        rows = direction[row : row + 8]
        total = total + rows * rows
    squares[...] = total

    @pl.when(part == pl.num_programs(0) - 1)
    def _():
        sumsq[0, 0] = jnp.sum(squares[...])


def direction_half(grad, momentum, n_col, lower, state):
    rows, n_in = grad.shape
    half, width = rows // 2, n_in // n_col
    parts = 2
    tile = pl.BlockSpec((half, n_in // parts), lambda j: (lower, j))
    filled = [] if state is None else [state]
    return pl.pallas_call(
        direction_kernel,
        grid=(parts,),
        in_specs=[tile, tile] + [pl.BlockSpec(memory_space=pl.ANY)] * len(filled),
        out_specs=[
            tile,
            pl.BlockSpec((n_col // parts, half, width), lambda j: (j, 0, 0)),
            pl.BlockSpec(memory_space=pltpu.SMEM),
        ],
        out_shape=[
            jax.ShapeDtypeStruct((rows, n_in), F32),
            jax.ShapeDtypeStruct((n_col, half, width), BF16),
            jax.ShapeDtypeStruct((1, 1), F32),
        ],
        input_output_aliases={2: 0} if filled else {},
        scratch_shapes=[pltpu.VMEM((8, n_in // parts), F32)],
        compiler_params=pltpu.CompilerParams(vmem_limit_bytes=VMEM),
    )(grad, momentum, *filled)


def direction_step(grad, momentum, n_col):
    rows, n_in = grad.shape
    half, width = rows // 2, n_in // n_col
    if half % 16:
        state = momentum_coef * momentum + grad
        direction = grad + momentum_coef * state
        raw = direction.astype(BF16).reshape(2, half, n_col, width).transpose(0, 2, 1, 3)
        return state, raw[0], raw[1], jnp.sum(direction * direction).reshape(1, 1)
    state, upper, upper_sum = direction_half(grad, momentum, n_col, 0, None)
    state, lower, lower_sum = direction_half(grad, momentum, n_col, 1, state)
    return state, upper, lower, upper_sum + lower_sum


def absorb_kernel(half, near_at, far_at, seeded, scaled, *refs):
    places, refs = refs[0], refs[1:]
    if scaled:
        scale, refs = refs[0], refs[1:]
    near, refs = refs[: len(near_at)], refs[len(near_at) :]
    far, refs = refs[: len(far_at)], refs[len(far_at) :]
    value, refs = refs[0], refs[1:]
    if seeded:
        before, refs = refs[0], refs[1:]
    block, total, refs = refs[0], refs[1], refs[2:]
    if scaled:
        rounded, refs = refs[0], refs[1:]
    turned, sems = refs
    tall = block.shape[0] // 2

    @pl.when(pl.program_id(0) == 0)
    def _():
        copies = []

        def place(source, target):
            copy = pltpu.make_async_copy(source, target, sems.at[len(copies)])
            copy.start()
            copies.append(copy)

        for k in range(len(near)):
            at = pl.ds(pl.multiple_of(places[k], 16), half)
            below = pl.ds(pl.multiple_of(places[k] + tall, 16), half)
            place(near[k].at[near_at[k]], block.at[at, pl.ds(0, tall)])
            place(near[k].at[near_at[k] + 1], block.at[below, pl.ds(tall, tall)])
            if not far:
                place(near[k].at[near_at[k] + 2], block.at[at, pl.ds(tall, tall)])
            else:
                place(far[k].at[far_at[k]], turned.at[0, at])
                place(far[k].at[far_at[k] + 1], turned.at[1, at])
        for copy in copies:
            copy.wait()
        for j in range(0, tall, 128):
            if not far:
                block[pl.ds(tall + j, 128), pl.ds(0, tall)] = block[
                    pl.ds(0, tall), pl.ds(tall + j, 128)
                ].T
            else:
                block[pl.ds(j, 128), pl.ds(tall, tall)] = turned[0, :, pl.ds(j, 128)].T
                block[pl.ds(tall + j, 128), pl.ds(0, tall)] = turned[1, :, pl.ds(j, 128)].T

    result = jnp.dot(block[...], value[...], preferred_element_type=F32)
    if seeded:
        result = result + before[...]
    if scaled:
        result = result * scale[0]
        rounded[...] = result.astype(BF16)
    total[...] = result


def absorb(places, near, far, value, wide, before=None, scale=None):
    _, half, tall = near[0][0].shape
    tile = min(TILE, wide)
    whole = pl.BlockSpec(memory_space=pl.ANY)
    scalars = pl.BlockSpec(memory_space=pltpu.SMEM)
    column = pl.BlockSpec((2 * tall, tile), lambda n: (0, n))
    operands, specs = [places], [scalars]
    if scale is not None:
        operands.append(scale)
        specs.append(scalars)
    operands += [*[piece for piece, _ in (*near, *far)], value]
    specs += [whole] * (len(near) + len(far)) + [column]
    if before is not None:
        operands.append(before)
        specs.append(column)
    shapes = [
        jax.ShapeDtypeStruct((2 * tall, 2 * tall), BF16),
        jax.ShapeDtypeStruct((2 * tall, wide), F32),
    ]
    out_specs = [pl.BlockSpec((2 * tall, 2 * tall), lambda n: (0, 0)), column]
    if scale is not None:
        shapes.append(jax.ShapeDtypeStruct((2 * tall, wide), BF16))
        out_specs.append(column)
    return pl.pallas_call(
        functools.partial(
            absorb_kernel,
            half,
            tuple(first for _, first in near),
            tuple(first for _, first in far),
            before is not None,
            scale is not None,
        ),
        grid=(wide // tile,),
        in_specs=specs,
        out_specs=out_specs,
        out_shape=shapes,
        scratch_shapes=[
            pltpu.VMEM((2, tall, tall), BF16),
            pltpu.SemaphoreType.DMA((4 * len(near),)),
        ],
        compiler_params=pltpu.CompilerParams(vmem_limit_bytes=VMEM),
        cost_estimate=pl.CostEstimate(
            flops=8 * tall * tall * wide, bytes_accessed=30 * tall * tall, transcendentals=0
        ),
    )(*operands)


def shards(grad, momentum):
    n_row, n_col = lax.axis_size("row"), lax.axis_size("col")
    n_ring = n_col // 2
    row, col = lax.axis_index("row"), lax.axis_index("col")
    ring, core = col // 2, col % 2
    rows, n_in = grad.shape
    half = rows // 2
    width = n_in // n_col
    tall = half * n_col
    m_total = rows * n_row * n_col
    slots = Slots()

    def after(value, *others):
        return lax.optimization_barrier((value, *others))[0]

    def across(value, distance):
        return lax.ppermute(value, "row", xor_pairs(n_row, distance))

    def other_core(value):
        return lax.ppermute(value, "col", xor_pairs(n_col, 1))

    def next_in_ring(value):
        return lax.ppermute(value, "col", shift_pairs(n_col, 2))

    new_momentum, *raw_halves, sumsq = direction_step(grad, momentum, n_col)

    sumsq = sumsq + other_core(sumsq)
    step = 1
    while step < n_row:
        sumsq = sumsq + across(sumsq, step)
        step *= 2
    raw_halves[1] = after(raw_halves[1], sumsq)

    near = (1, 2) if n_row == 4 else tuple(range(1, n_row))
    own = []
    for h in range(2):
        block = lax.all_to_all(raw_halves[h], "col", split_axis=0, concat_axis=0)
        own.append(block.reshape(tall, width))
        if h == 0:
            others = [{d: across(own[0], d) for d in near}, {}]
    own[1] = after(own[1], *others[0].values())
    own2 = jnp.stack(own)
    cut = tall * 3 // 4

    def is_upper(d):
        return ((row >> low_bit(d)) & 1) == 1

    def swapped(first_half, second_half, d):
        return jnp.stack(
            [
                jnp.where(is_upper(d), second_half, first_half),
                jnp.where(is_upper(d), first_half, second_half),
            ]
        )

    own2 = jnp.stack(own)
    mixed = {}

    def gram_term(left, right):
        return lax.dot_general(
            left, right, (((2,), (2,)), ((0,), (0,))), preferred_element_type=F32
        ).astype(BF16)

    class Reduce:
        def __init__(self, terms):
            self.pieces = [term.reshape(-1, n_ring, 2, half, tall) for term in terms]
            self.parts = [self.part(t) for t in range(n_ring)]
            self.done = 0
            self.total = self.parts[0].astype(BF16)

        def part(self, t):
            index = (ring + n_ring - 1 - t) % n_ring
            sent, kept = self.pick(index, 1 - core), self.pick(index, core)
            return slots.note(kept.astype(F32) + other_core(sent).astype(F32))

        def pick(self, index, which):
            zero = jnp.zeros((), jnp.int32)
            picked = []
            for piece in self.pieces:
                sizes = (piece.shape[0], 1, 1, half, tall)
                part = lax.dynamic_slice(slots.hold(piece), (zero, index, which, zero, zero), sizes)
                picked.append(part.reshape(-1, half, tall))
            return picked[0] if len(picked) == 1 else jnp.concatenate(picked)

        def step(self):
            self.done += 1
            moved = slots.note(next_in_ring(slots.hold(self.total)))
            self.total = (moved.astype(F32) + self.parts[self.done]).astype(BF16)

    class Gather:
        def __init__(self, piece, distances):
            self.distances = distances
            self.found, self.partner = [piece], []
            self.crossed = {d: ([], []) for d in distances}
            self.left = list(enumerate(distances)) or [(0, 0)]

        @property
        def taken(self):
            return not self.left

        def complete(self):
            shared = [self.partner, *[theirs for _, theirs in self.crossed.values()]]
            return all(len(pieces) == n_ring for pieces in shared)

        def take_next(self, total, scale=None):
            i, d = self.left.pop(0)
            near = [(piece, 2 * i) for piece in self.found]
            near += [(piece, at + 2 * i) for piece, at in self.partner]
            far = self.crossed[d][0] + self.crossed[d][1] if d else []
            value = flat(mixed[d] if d else own2)
            blocks[d], *made = take(near, far, value, total, None if self.left else scale)
            return made[0], made[1:]

        def step(self):
            self.found.append(slots.note(next_in_ring(slots.hold(self.found[-1]))))

        def swaps(self):
            wanted = []
            for mine, theirs in self.crossed.values():
                wanted += [(part[at : at + 2], theirs) for part, at in mine[len(theirs) :]]
            return wanted + [(piece, self.partner) for piece in self.found[len(self.partner) :]]

        def cross(self):
            for i, d in enumerate(self.distances):
                mine = self.crossed[d][0]
                parts = []
                for piece in self.found[len(mine) :]:
                    part = slots.hold(piece[2 * i : 2 * i + 2])
                    parts.append(jnp.where(is_upper(d), jnp.flip(part, 0), part))
                if parts:
                    moved = across(jnp.concatenate(parts) if parts[1:] else parts[0], d)
                    mine += [(slots.note(moved), 2 * k) for k in range(len(parts))]

    def share(gathers, crossing=True):
        wanted = [pair for gather in gathers for pair in gather.swaps()]
        if wanted:
            parts = [slots.hold(part) for part, _ in wanted]
            swapped_parts = slots.note(other_core(jnp.concatenate(parts) if parts[1:] else parts[0]))
            at = 0
            for part, answers in wanted:
                answers.append((swapped_parts, at))
                at += part.shape[0]
        for gather in gathers if crossing else ():
            gather.cross()

    places = [(ring - k + n_ring) % n_ring for k in range(n_ring)]
    places = [(2 * place + core) * half for place in places] + [
        (2 * place + 1 - core) * half for place in places
    ]
    places = jnp.stack(places).astype(jnp.int32)
    n_in_line = 2 * tall
    wide = width // 2
    aligned = half % 16 == 0 and tall % 128 == 0

    def take(near, far, value, before=None, scale=None):
        if aligned:
            return absorb(places, near, far, value, wide, before, scale)

        def tiles(pieces, count):
            full = jnp.zeros((count, tall, tall), BF16)
            for k, (piece, at) in enumerate(pieces):
                full = lax.dynamic_update_slice(full, piece[at : at + count], (0, places[k], 0))
            return full

        near = tiles(near, 2 if far else 3)
        b, c = tiles(far, 2).transpose(0, 2, 1) if far else (near[2], near[2].T)
        block = jnp.concatenate(
            [jnp.concatenate([near[0], b], axis=1), jnp.concatenate([c, near[1]], axis=1)], axis=0
        )
        block = lax.optimization_barrier(block)
        total = jnp.dot(block, value[:, :wide], preferred_element_type=F32)
        total = total if before is None else total + before
        if scale is None:
            return block, total
        total = total * scale[0]
        return block, total, total.astype(BF16)

    def flat(value):
        return value.reshape(n_in_line, value.shape[-1])

    distances = list(range(1, n_row))
    groups = [distances[i : i + 2] for i in range(0, len(distances), 2)]
    blocks = {}
    moving = {}

    def move_second_half(part):
        for d in near:
            moving[d, part] = slots.note(across(slots.hold(own[1][part]), d))

    def move_to_diagonal(part):
        if n_row == 4:
            one, two = slots.hold(others[0][1][part]), slots.hold(moving[2, part])
            moving[3, 0, part] = slots.note(across(one, 2))
            moving[3, 1, part] = slots.note(across(two, 1))

    def make_term(d):
        if d in near:
            lower = jnp.concatenate([moving[d, part] for part in parts])
            upper = others[0][d]
        else:
            upper, lower = [jnp.concatenate([moving[3, h, part] for part in parts]) for h in range(2)]
        mixed[d] = swapped(slots.hold(upper), slots.hold(lower), d)
        return slots.note(gram_term(own2, mixed[d]))

    parts = (slice(0, cut), slice(cut, tall))
    move_second_half(parts[0])
    sumsq = after(sumsq, own[1])
    step = 2
    while step < n_col:
        sumsq = sumsq + lax.ppermute(sumsq, "col", xor_pairs(n_col, step))
        step *= 2
    slots.note(sumsq)
    reduces = [[Reduce([gram_term(own2, own2), gram_term(own2[:1], own2[1:])]), []]]
    slots.close()
    gathers, terms = [], {}
    total, rounded = None, None
    waiting = [(d, 3 if d in near else 5) for d in distances]
    number = 2
    while reduces or waiting or terms or any(len(g.found) < n_ring for g in gathers):
        if number == 2:
            move_second_half(parts[1])
        elif number in (3, 4):
            move_to_diagonal(parts[number - 3])
        stepping = [run for run, _ in reduces][:2]
        stepping += [g for g in gathers if g.distances and len(g.found) < n_ring][: 2 - len(stepping)]
        stepping += [g for g in gathers if not g.distances and len(g.found) < n_ring]
        share(gathers, len(stepping) <= 2)
        for run in stepping:
            run.step()
        opened = None
        if groups and number >= 3:
            for group in groups[:1]:
                if all(d in terms for d in group):
                    opened = [Reduce([terms.pop(d) for d in group]), groups.pop(0)]
                    opened[0].step()
        while waiting and number >= waiting[0][1]:
            d = waiting.pop(0)[0]
            terms[d] = make_term(d)
        complete = [gather for gather in gathers if gather.complete() and not gather.taken]
        if complete and (groups or reduces or gathers[-1] is not complete[0]):
            total, rounded = complete[0].take_next(total)
            slots.note(total)
        slots.close()
        for pair in [pair for pair in reduces if pair[0].done == n_ring - 1]:
            gathers.append(Gather(pair[0].total, pair[1]))
            reduces.remove(pair)
        if opened:
            reduces.append(opened)
        number += 1
    factor = rms_target * math.sqrt(m_total) / (jnp.sqrt(sumsq) + 1e-07)
    factor_sq = factor * factor
    scale = factor_sq.reshape(1)
    share(gathers)
    for gather in gathers[:-1]:
        if not gather.taken and gather.complete():
            total, rounded = gather.take_next(total)
            slots.note(total)
    slots.close()
    share(gathers)
    for gather in gathers:
        while not gather.taken:
            total, rounded = gather.take_next(total, scale if gather is gathers[-1] else None)

    def product(d, value):
        return jnp.dot(blocks[d], value, preferred_element_type=F32)

    left, right = slice(0, wide), slice(wide, 2 * wide)
    last = 0.0
    for d in [0, *distances]:
        value = after(flat(mixed[d] if d else own2), rounded[0])
        last = last + product(d, value[:, right])
    first = [total, last * factor_sq]
    rounds = [rounded[0].reshape(2, tall, wide), first[1].astype(BF16).reshape(2, tall, wide)]
    scale_out = 0.2 * math.sqrt(max(m_total, n_in))
    def send(value, *ties):
        value = after(value, *ties) if ties else value
        return {d: across(value, d) for d in near}

    def forward(found, tie):
        if n_row != 4:
            return ()
        one, two = after(found[1][0], tie), after(found[2][1], tie)
        return across(one, 2), across(two, 1)

    def nearby(value, found, tie, later=False):
        second = product(0, flat(after(value, tie)))
        for d in near[:-1] if later else near:
            second = second + product(d, flat(swapped(*[after(v, tie) for v in found[d]], d)))
        return second

    def finish(side, second, corner, *ties):
        if side == 0:
            d = near[-1]
            halves = [after(v, *ties) for v in found[0][d]]
            second = second + product(d, flat(swapped(*halves, d)))
        if corner:
            second = second + product(3, flat(swapped(*[after(v, *ties) for v in corner], 3)))
        mine = flat(own2)[:, (left, right)[side]].astype(F32)
        result = coef_a * mine + coef_b * first[side] + coef_c * (second * factor_sq)
        return (result * (factor * scale_out)).astype(BF16).reshape(2, n_col, half, wide)

    def send_back(block):
        return lax.all_to_all(block, "col", split_axis=1, concat_axis=1, tiled=True)

    found = [send(rounds[0])]
    ended = lax.optimization_barrier((rounds[1], *found[0].values()))[0]
    corner = forward(found[0], ended)
    second = nearby(rounds[0], found[0], ended, True)
    ended = lax.optimization_barrier((second, *corner))[0]
    found.append(send(rounds[1], ended))
    block = finish(0, second, corner, ended)
    ended = lax.optimization_barrier((block, *found[1].values()))[0]
    backs = [send_back(block)]
    corner = forward(found[1], ended)
    second = nearby(rounds[1], found[1], ended)
    ended = lax.optimization_barrier((second, backs[0], *corner))[0]
    backs.append(send_back(finish(1, second, corner, ended)))
    update = jnp.zeros((rows, n_in), BF16)
    for side, back in enumerate(backs):
        for source in range(n_col):
            piece = back[:, source].reshape(rows, wide)
            update = lax.dynamic_update_slice(update, piece, (0, source * width + side * wide))
    return (update, new_momentum)


def solution(mesh):
    return jax.shard_map(
        shards,
        mesh=mesh,
        in_specs=(P(("row", "col"), None), P(("row", "col"), None)),
        out_specs=(P(("row", "col"), None), P(("row", "col"), None)),
        check_vma=False,
    )
```

```python
import math

import functools

import jax
import jax.numpy as jnp
from jax import lax
from jax.experimental import pallas as pl
from jax.experimental.pallas import tpu as pltpu
from jax.sharding import PartitionSpec as P

momentum_coef = 0.95
rms_target = 0.4
coef_a = 3.4445
coef_b = -4.775
coef_c = 2.0315
TILE = 256
VMEM = 56 * 1024 * 1024
F32 = jnp.float32
BF16 = jnp.bfloat16


def xor_pairs(size, distance):
    return [(i, i ^ distance) for i in range(size)]


def shift_pairs(size, distance):
    return [(i, (i + distance) % size) for i in range(size)]


def low_bit(distance):
    return (distance & -distance).bit_length() - 1


class Slots:
    def __init__(self):
        self.ended, self.noted = None, []

    def hold(self, value):
        return value if self.ended is None else lax.optimization_barrier((value, self.ended))[0]

    def note(self, value):
        self.noted.append(value)
        return value

    def close(self):
        if self.noted:
            self.ended = lax.optimization_barrier(tuple(self.noted))[0]
            self.noted = []


def direction_kernel(grad, momentum, *refs):
    new_momentum, raw, sumsq, squares = refs[-4:]
    part = pl.program_id(0)
    state = momentum_coef * momentum[...] + grad[...]
    new_momentum[...] = state
    direction = grad[...] + momentum_coef * state
    width = raw.shape[2]
    for group in range(raw.shape[0]):
        raw[group] = direction[:, group * width : (group + 1) * width].astype(BF16)

    @pl.when(part == 0)
    def _():
        squares[...] = jnp.zeros_like(squares)

    total = squares[...]
    for row in range(0, direction.shape[0], 8):
        rows = direction[row : row + 8]
        total = total + rows * rows
    squares[...] = total

    @pl.when(part == pl.num_programs(0) - 1)
    def _():
        sumsq[0, 0] = jnp.sum(squares[...])


def direction_half(grad, momentum, n_col, lower, state):
    rows, n_in = grad.shape
    half, width = rows // 2, n_in // n_col
    parts = 2
    tile = pl.BlockSpec((half, n_in // parts), lambda j: (lower, j))
    filled = [] if state is None else [state]
    return pl.pallas_call(
        direction_kernel,
        grid=(parts,),
        in_specs=[tile, tile] + [pl.BlockSpec(memory_space=pl.ANY)] * len(filled),
        out_specs=[
            tile,
            pl.BlockSpec((n_col // parts, half, width), lambda j: (j, 0, 0)),
            pl.BlockSpec(memory_space=pltpu.SMEM),
        ],
        out_shape=[
            jax.ShapeDtypeStruct((rows, n_in), F32),
            jax.ShapeDtypeStruct((n_col, half, width), BF16),
            jax.ShapeDtypeStruct((1, 1), F32),
        ],
        input_output_aliases={2: 0} if filled else {},
        scratch_shapes=[pltpu.VMEM((8, n_in // parts), F32)],
        compiler_params=pltpu.CompilerParams(vmem_limit_bytes=VMEM),
    )(grad, momentum, *filled)


def direction_step(grad, momentum, n_col):
    rows, n_in = grad.shape
    half, width = rows // 2, n_in // n_col
    if half % 16:
        state = momentum_coef * momentum + grad
        direction = grad + momentum_coef * state
        raw = direction.astype(BF16).reshape(2, half, n_col, width).transpose(0, 2, 1, 3)
        return state, raw[0], raw[1], jnp.sum(direction * direction).reshape(1, 1)
    state, upper, upper_sum = direction_half(grad, momentum, n_col, 0, None)
    state, lower, lower_sum = direction_half(grad, momentum, n_col, 1, state)
    return state, upper, lower, upper_sum + lower_sum


def absorb_kernel(half, near_at, far_at, seeded, scaled, *refs):
    places, refs = refs[0], refs[1:]
    if scaled:
        scale, refs = refs[0], refs[1:]
    near, refs = refs[: len(near_at)], refs[len(near_at) :]
    far, refs = refs[: len(far_at)], refs[len(far_at) :]
    value, refs = refs[0], refs[1:]
    if seeded:
        before, refs = refs[0], refs[1:]
    block, total, refs = refs[0], refs[1], refs[2:]
    if scaled:
        rounded, refs = refs[0], refs[1:]
    turned, sems = refs
    tall = block.shape[0] // 2

    @pl.when(pl.program_id(0) == 0)
    def _():
        copies = []

        def place(source, target):
            copy = pltpu.make_async_copy(source, target, sems.at[len(copies)])
            copy.start()
            copies.append(copy)

        for k in range(len(near)):
            at = pl.ds(pl.multiple_of(places[k], 16), half)
            below = pl.ds(pl.multiple_of(places[k] + tall, 16), half)
            place(near[k].at[near_at[k]], block.at[at, pl.ds(0, tall)])
            place(near[k].at[near_at[k] + 1], block.at[below, pl.ds(tall, tall)])
            if not far:
                place(near[k].at[near_at[k] + 2], block.at[at, pl.ds(tall, tall)])
            else:
                place(far[k].at[far_at[k]], turned.at[0, at])
                place(far[k].at[far_at[k] + 1], turned.at[1, at])
        for copy in copies:
            copy.wait()
        for j in range(0, tall, 128):
            if not far:
                block[pl.ds(tall + j, 128), pl.ds(0, tall)] = block[
                    pl.ds(0, tall), pl.ds(tall + j, 128)
                ].T
            else:
                block[pl.ds(j, 128), pl.ds(tall, tall)] = turned[0, :, pl.ds(j, 128)].T
                block[pl.ds(tall + j, 128), pl.ds(0, tall)] = turned[1, :, pl.ds(j, 128)].T

    result = jnp.dot(block[...], value[...], preferred_element_type=F32)
    if seeded:
        result = result + before[...]
    if scaled:
        result = result * scale[0]
        rounded[...] = result.astype(BF16)
    total[...] = result


def absorb(places, near, far, value, wide, before=None, scale=None):
    _, half, tall = near[0][0].shape
    tile = min(TILE, wide)
    whole = pl.BlockSpec(memory_space=pl.ANY)
    scalars = pl.BlockSpec(memory_space=pltpu.SMEM)
    column = pl.BlockSpec((2 * tall, tile), lambda n: (0, n))
    operands, specs = [places], [scalars]
    if scale is not None:
        operands.append(scale)
        specs.append(scalars)
    operands += [*[piece for piece, _ in (*near, *far)], value]
    specs += [whole] * (len(near) + len(far)) + [column]
    if before is not None:
        operands.append(before)
        specs.append(column)
    shapes = [
        jax.ShapeDtypeStruct((2 * tall, 2 * tall), BF16),
        jax.ShapeDtypeStruct((2 * tall, wide), F32),
    ]
    out_specs = [pl.BlockSpec((2 * tall, 2 * tall), lambda n: (0, 0)), column]
    if scale is not None:
        shapes.append(jax.ShapeDtypeStruct((2 * tall, wide), BF16))
        out_specs.append(column)
    return pl.pallas_call(
        functools.partial(
            absorb_kernel,
            half,
            tuple(first for _, first in near),
            tuple(first for _, first in far),
            before is not None,
            scale is not None,
        ),
        grid=(wide // tile,),
        in_specs=specs,
        out_specs=out_specs,
        out_shape=shapes,
        scratch_shapes=[
            pltpu.VMEM((2, tall, tall), BF16),
            pltpu.SemaphoreType.DMA((4 * len(near),)),
        ],
        compiler_params=pltpu.CompilerParams(vmem_limit_bytes=VMEM),
        cost_estimate=pl.CostEstimate(
            flops=8 * tall * tall * wide, bytes_accessed=30 * tall * tall, transcendentals=0
        ),
    )(*operands)


def shards(grad, momentum):
    n_row, n_col = lax.axis_size("row"), lax.axis_size("col")
    n_ring = n_col // 2
    row, col = lax.axis_index("row"), lax.axis_index("col")
    ring, core = col // 2, col % 2
    rows, n_in = grad.shape
    half = rows // 2
    width = n_in // n_col
    tall = half * n_col
    m_total = rows * n_row * n_col
    slots = Slots()

    def after(value, *others):
        return lax.optimization_barrier((value, *others))[0]

    def across(value, distance):
        return lax.ppermute(value, "row", xor_pairs(n_row, distance))

    def other_core(value):
        return lax.ppermute(value, "col", xor_pairs(n_col, 1))

    def next_in_ring(value):
        return lax.ppermute(value, "col", shift_pairs(n_col, 2))

    new_momentum, *raw_halves, sumsq = direction_step(grad, momentum, n_col)

    sumsq = sumsq + other_core(sumsq)
    step = 1
    while step < n_row:
        sumsq = sumsq + across(sumsq, step)
        step *= 2
    raw_halves[1] = after(raw_halves[1], sumsq)

    near = (1, 2) if n_row == 4 else tuple(range(1, n_row))
    own = []
    for h in range(2):
        block = lax.all_to_all(raw_halves[h], "col", split_axis=0, concat_axis=0)
        own.append(block.reshape(tall, width))
        if h == 0:
            others = [{d: across(own[0], d) for d in near}, {}]
    own[1] = after(own[1], *others[0].values())
    own2 = jnp.stack(own)
    cut = tall // 2

    def is_upper(d):
        return ((row >> low_bit(d)) & 1) == 1

    def swapped(first_half, second_half, d):
        return jnp.stack(
            [
                jnp.where(is_upper(d), second_half, first_half),
                jnp.where(is_upper(d), first_half, second_half),
            ]
        )

    own2 = jnp.stack(own)
    mixed = {}

    def gram_term(left, right):
        return lax.dot_general(
            left, right, (((2,), (2,)), ((0,), (0,))), preferred_element_type=F32
        ).astype(BF16)

    class Reduce:
        def __init__(self, terms):
            self.pieces = [term.reshape(-1, n_ring, 2, half, tall) for term in terms]
            self.parts = [self.part(t) for t in range(n_ring)]
            self.done = 0
            self.total = self.parts[0].astype(BF16)

        def part(self, t):
            index = (ring + n_ring - 1 - t) % n_ring
            sent, kept = self.pick(index, 1 - core), self.pick(index, core)
            return slots.note(kept.astype(F32) + other_core(sent).astype(F32))

        def pick(self, index, which):
            zero = jnp.zeros((), jnp.int32)
            picked = []
            for piece in self.pieces:
                sizes = (piece.shape[0], 1, 1, half, tall)
                part = lax.dynamic_slice(slots.hold(piece), (zero, index, which, zero, zero), sizes)
                picked.append(part.reshape(-1, half, tall))
            return picked[0] if len(picked) == 1 else jnp.concatenate(picked)

        def step(self):
            self.done += 1
            moved = slots.note(next_in_ring(slots.hold(self.total)))
            self.total = (moved.astype(F32) + self.parts[self.done]).astype(BF16)

    class Gather:
        def __init__(self, piece, distances):
            self.distances = distances
            self.found, self.partner = [piece], []
            self.crossed = {d: ([], []) for d in distances}
            self.left = list(enumerate(distances)) or [(0, 0)]

        @property
        def taken(self):
            return not self.left

        def complete(self):
            shared = [self.partner, *[theirs for _, theirs in self.crossed.values()]]
            return all(len(pieces) == n_ring for pieces in shared)

        def take_next(self, total, scale=None):
            i, d = self.left.pop(0)
            near = [(piece, 2 * i) for piece in self.found]
            near += [(piece, at + 2 * i) for piece, at in self.partner]
            far = self.crossed[d][0] + self.crossed[d][1] if d else []
            value = flat(mixed[d] if d else own2)
            blocks[d], *made = take(near, far, value, total, None if self.left else scale)
            return made[0], made[1:]

        def step(self):
            self.found.append(slots.note(next_in_ring(slots.hold(self.found[-1]))))

        def swaps(self):
            wanted = []
            for mine, theirs in self.crossed.values():
                wanted += [(part[at : at + 2], theirs) for part, at in mine[len(theirs) :]]
            return wanted + [(piece, self.partner) for piece in self.found[len(self.partner) :]]

        def cross(self):
            for i, d in enumerate(self.distances):
                mine = self.crossed[d][0]
                parts = []
                for piece in self.found[len(mine) :]:
                    part = slots.hold(piece[2 * i : 2 * i + 2])
                    parts.append(jnp.where(is_upper(d), jnp.flip(part, 0), part))
                if parts:
                    moved = across(jnp.concatenate(parts) if parts[1:] else parts[0], d)
                    mine += [(slots.note(moved), 2 * k) for k in range(len(parts))]

    def share(gathers, crossing=True):
        wanted = [pair for gather in gathers for pair in gather.swaps()]
        if wanted:
            parts = [slots.hold(part) for part, _ in wanted]
            swapped_parts = slots.note(other_core(jnp.concatenate(parts) if parts[1:] else parts[0]))
            at = 0
            for part, answers in wanted:
                answers.append((swapped_parts, at))
                at += part.shape[0]
        for gather in gathers if crossing else ():
            gather.cross()

    places = [(ring - k + n_ring) % n_ring for k in range(n_ring)]
    places = [(2 * place + core) * half for place in places] + [
        (2 * place + 1 - core) * half for place in places
    ]
    places = jnp.stack(places).astype(jnp.int32)
    n_in_line = 2 * tall
    wide = width // 2
    aligned = half % 16 == 0 and tall % 128 == 0

    def take(near, far, value, before=None, scale=None):
        if aligned:
            return absorb(places, near, far, value, wide, before, scale)

        def tiles(pieces, count):
            full = jnp.zeros((count, tall, tall), BF16)
            for k, (piece, at) in enumerate(pieces):
                full = lax.dynamic_update_slice(full, piece[at : at + count], (0, places[k], 0))
            return full

        near = tiles(near, 2 if far else 3)
        b, c = tiles(far, 2).transpose(0, 2, 1) if far else (near[2], near[2].T)
        block = jnp.concatenate(
            [jnp.concatenate([near[0], b], axis=1), jnp.concatenate([c, near[1]], axis=1)], axis=0
        )
        block = lax.optimization_barrier(block)
        total = jnp.dot(block, value[:, :wide], preferred_element_type=F32)
        total = total if before is None else total + before
        if scale is None:
            return block, total
        total = total * scale[0]
        return block, total, total.astype(BF16)

    def flat(value):
        return value.reshape(n_in_line, value.shape[-1])

    distances = list(range(1, n_row))
    groups = [distances[i : i + 2] for i in range(0, len(distances), 2)]
    blocks = {}
    moving = {}

    def move_second_half(part):
        for d in near:
            moving[d, part] = slots.note(across(slots.hold(own[1][part]), d))

    def move_to_diagonal(part):
        if n_row == 4:
            one, two = slots.hold(others[0][1][part]), slots.hold(moving[2, part])
            moving[3, 0, part] = slots.note(across(one, 2))
            moving[3, 1, part] = slots.note(across(two, 1))

    def make_term(d):
        if d in near:
            lower = jnp.concatenate([moving[d, part] for part in parts])
            upper = others[0][d]
        else:
            upper, lower = [jnp.concatenate([moving[3, h, part] for part in parts]) for h in range(2)]
        mixed[d] = swapped(slots.hold(upper), slots.hold(lower), d)
        return slots.note(gram_term(own2, mixed[d]))

    parts = (slice(0, cut), slice(cut, tall))
    move_second_half(parts[0])
    sumsq = after(sumsq, own[1])
    step = 2
    while step < n_col:
        sumsq = sumsq + lax.ppermute(sumsq, "col", xor_pairs(n_col, step))
        step *= 2
    slots.note(sumsq)
    reduces = [[Reduce([gram_term(own2, own2), gram_term(own2[:1], own2[1:])]), []]]
    slots.close()
    gathers, terms = [], {}
    total, rounded = None, None
    waiting = [(d, 3 if d in near else 5) for d in distances]
    number = 2
    while reduces or waiting or terms or any(len(g.found) < n_ring for g in gathers):
        if number == 2:
            move_second_half(parts[1])
        elif number in (3, 4):
            move_to_diagonal(parts[number - 3])
        stepping = [run for run, _ in reduces][:2]
        stepping += [g for g in gathers if g.distances and len(g.found) < n_ring][: 2 - len(stepping)]
        stepping += [g for g in gathers if not g.distances and len(g.found) < n_ring]
        share(gathers, len(stepping) <= 2)
        for run in stepping:
            run.step()
        opened = None
        if groups and number >= 3:
            for group in groups[:1]:
                if all(d in terms for d in group):
                    opened = [Reduce([terms.pop(d) for d in group]), groups.pop(0)]
                    opened[0].step()
        while waiting and number >= waiting[0][1]:
            d = waiting.pop(0)[0]
            terms[d] = make_term(d)
        complete = [gather for gather in gathers if gather.complete() and not gather.taken]
        if complete and (groups or reduces or gathers[-1] is not complete[0]):
            total, rounded = complete[0].take_next(total)
            slots.note(total)
        slots.close()
        for pair in [pair for pair in reduces if pair[0].done == n_ring - 1]:
            gathers.append(Gather(pair[0].total, pair[1]))
            reduces.remove(pair)
        if opened:
            reduces.append(opened)
        number += 1
    factor = rms_target * math.sqrt(m_total) / (jnp.sqrt(sumsq) + 1e-07)
    factor_sq = factor * factor
    scale = factor_sq.reshape(1)
    share(gathers)
    for gather in gathers[:-1]:
        if not gather.taken and gather.complete():
            total, rounded = gather.take_next(total)
            slots.note(total)
    slots.close()
    share(gathers)
    for gather in gathers:
        while not gather.taken:
            total, rounded = gather.take_next(total, scale if gather is gathers[-1] else None)

    def product(d, value):
        return jnp.dot(blocks[d], value, preferred_element_type=F32)

    left, right = slice(0, wide), slice(wide, 2 * wide)
    last = 0.0
    for d in [0, *distances]:
        value = after(flat(mixed[d] if d else own2), rounded[0])
        last = last + product(d, value[:, right])
    first = [total, last * factor_sq]
    rounds = [rounded[0].reshape(2, tall, wide), first[1].astype(BF16).reshape(2, tall, wide)]
    scale_out = 0.2 * math.sqrt(max(m_total, n_in))
    def send(value, *ties):
        value = after(value, *ties) if ties else value
        return {d: across(value, d) for d in near}

    def forward(found, tie):
        if n_row != 4:
            return ()
        one, two = after(found[1][0], tie), after(found[2][1], tie)
        return across(one, 2), across(two, 1)

    def nearby(value, found, tie, later=False):
        second = product(0, flat(after(value, tie)))
        for d in near[:-1] if later else near:
            second = second + product(d, flat(swapped(*[after(v, tie) for v in found[d]], d)))
        return second

    def finish(side, second, corner, *ties):
        if side == 0:
            d = near[-1]
            halves = [after(v, *ties) for v in found[0][d]]
            second = second + product(d, flat(swapped(*halves, d)))
        if corner:
            second = second + product(3, flat(swapped(*[after(v, *ties) for v in corner], 3)))
        mine = flat(own2)[:, (left, right)[side]].astype(F32)
        result = coef_a * mine + coef_b * first[side] + coef_c * (second * factor_sq)
        return (result * (factor * scale_out)).astype(BF16).reshape(2, n_col, half, wide)

    def send_back(block):
        return lax.all_to_all(block, "col", split_axis=1, concat_axis=1, tiled=True)

    found = [send(rounds[0])]
    ended = lax.optimization_barrier((rounds[1], *found[0].values()))[0]
    corner = forward(found[0], ended)
    second = nearby(rounds[0], found[0], ended, True)
    ended = lax.optimization_barrier((second, *corner))[0]
    found.append(send(rounds[1], ended))
    block = finish(0, second, corner, ended)
    ended = lax.optimization_barrier((block, *found[1].values()))[0]
    backs = [send_back(block)]
    corner = forward(found[1], ended)
    second = nearby(rounds[1], found[1], ended)
    ended = lax.optimization_barrier((second, backs[0], *corner))[0]
    block = finish(1, second, corner, ended)
    update = jnp.zeros((rows, n_in), BF16)
    for side, back in enumerate(backs):
        for source in range(n_col):
            piece = back[:, source].reshape(rows, wide)
            update = lax.dynamic_update_slice(update, piece, (0, source * width + side * wide))
    for k in range(n_col):
        piece = lax.dynamic_index_in_dim(block, (col + k) % n_col, 1, keepdims=False)
        if k:
            piece = lax.ppermute(piece, "col", shift_pairs(n_col, k))
        source = (col - k + n_col) % n_col
        update = lax.dynamic_update_slice(
            update, piece.reshape(rows, -1), (0, source * width + wide)
        )
    return (update, new_momentum)


def solution(mesh):
    return jax.shard_map(
        shards,
        mesh=mesh,
        in_specs=(P(("row", "col"), None), P(("row", "col"), None)),
        out_specs=(P(("row", "col"), None), P(("row", "col"), None)),
        check_vma=False,
    )
```
